512 devices in a mesh: sec: 2 (over core), sp: 4 (over y), dev: 64 (over x, z).
Axes of the slice: x: 4, y: 4, z: 16, core: 2. Of those that a mesh axis runs over, the one named last changes fastest.
Arguments:
- patch_qkv: bfloat16 [65536, 3, 1280], P(('sec', 'sp', 'dev')), may hold values from -13 to 13
- patch_state: bfloat16 [65536, 1280], P(('sec', 'sp', 'dev')), may hold values from -6 to 6
- window_index: int32 [512, 128], P(('sec', 'sp', 'dev')), may hold values from 0 to 127, each once within a row
- patch_owner: int32 [65536, 1], P(('sec', 'sp', 'dev')), may hold values from 0 to 127; in each aligned block of 128 rows (0 to 127, 128 to 255, ...) at most 2 rows name the same one
- source_request: int32 [128, 128], P(('sec', 'dev')), may hold values from 0 to 7, never falling along the last dimension, each value on 1 to 64 neighbouring positions
- norm_gain: float32 [1280], replicated, may hold values from 0.1 to 1.9
- w_qkv: bfloat16 [1280, 3, 1280], P(None, None, 'sp'), may hold values from -0.15625 to 0.15625
- b_qkv: bfloat16 [3, 1280], P(None, 'sp'), may hold values from -12 to 12
Outputs:
- out_rows: bfloat16 [65536, 1280], P(('sec', 'sp', 'dev'))
The draws below stay inside these ranges and needn't reach their ends.
Inputs may be any that keep to these rules, and one draw needn't show every extreme that they name: `window_index`: each row is a permutation of the 128 local patch indices of one device. `patch_owner`: among the 128 patches of one device no owner is named more than 2 times, and on some device one owner is named exactly 2 times. `source_request`: along each row the request number never falls; each request covers 1 to 64 consecutive source positions, one exactly 64.
All inputs are finite; a program needn't handle non-finite values.
Results may differ from the reference program's by a relative error of at most 0.012.
The reference program's roundings to bfloat16 on the way (of `window_out`, `moved`, `group_rows`, `normed`, `projected`, `weights` and `mixed`) count: a program that leaves them out, or rounds other values in their place, can miss the bound.
Values may be sent and summed in bfloat16 or wider, within the bound.
A program may use at most 64 MiB of HBM per device.

```python
import math
import jax
import jax.numpy as jnp
import numpy as np
from jax import lax

HV = 1280
HEADS = 16
HD = 80
WIN = 64
P_DEV = 128
OWNERS = 128
CAP = 2
REQS = 8
RMOST = 64
PATCHES = 65536
N_SEC = 2
N_SP = 4
N_DEV = 64


def draw_patch_qkv(key, part):
    noise_key = jax.random.fold_in(key, 0)
    values = jax.random.truncated_normal(noise_key, -6.0, 6.0, (PATCHES, 3, HV), jnp.float32)
    return values.astype(jnp.bfloat16)


def draw_b_qkv(key, part):
    noise_key = jax.random.fold_in(key, 0)
    values = 0.3 * jax.random.truncated_normal(noise_key, -6.5, 6.5, (3, HV), jnp.float32)
    return values.astype(jnp.bfloat16)


def level_of(own_key, dims, pieces, smallest, top_value):
    loudness, own = 1.0, jax.random.fold_in(own_key, 6)
    for position, blocks in pieces:
        steps = jnp.exp(jax.random.uniform(jax.random.fold_in(own, position), (blocks,), jnp.float32, smallest / len(pieces), top_value / len(pieces)))
        loudness = loudness * jnp.repeat(steps, dims[position] // blocks).reshape([-1 if axis == position else 1 for axis in range(len(dims))])
    return loudness


def split_up(amount, total, limit, skew):
    loads = [(1 << 20) // math.isqrt(rank ** skew) + 1 for rank in range(2, amount + 1)]
    surplus, counts = total - limit - (amount - 1), [1] * (amount - 1)
    while surplus > 0:
        free = [i for i in range(amount - 1) if counts[i] < limit]
        mass, remaining = sum([loads[i] for i in free]), surplus
        for i in free:
            more = min(limit - counts[i], max(1, remaining * loads[i] // mass), surplus)
            counts[i] = counts[i] + more
            surplus = surplus - more
    return np.array([limit] + counts)


def ragged_sizes(own_key, amount, total, most, slope):
    if amount == 2:
        one = jax.random.randint(own_key, (), max(1, total - most), min(most, total - 1) + 1)
        return jnp.stack([one, total - one])
    lengths = jnp.asarray(split_up(amount, total, most, slope), jnp.int32)
    twos = (amount - 1) // 2
    giver, taker = lengths[1:1 + 2 * twos:2], lengths[2:2 + 2 * twos:2]
    room = jnp.minimum(giver - 1, most - taker)
    passed = jax.random.randint(jax.random.fold_in(own_key, 1), (twos,), 0, 1 << 20) % (room + 1)
    lengths = lengths.at[1:1 + 2 * twos:2].set(giver - passed).at[2:2 + 2 * twos:2].set(taker + passed)
    return lengths[jax.random.permutation(jax.random.fold_in(own_key, 2), amount)]


def shared_out(key, own, number, rows, amount, top, reach, lean):
    sequence = jax.random.permutation(key, amount)
    packed, common = portions_of(amount, rows * top, reach, lean, True), portions_of(amount, rows * top, reach, lean, False)
    places = jnp.arange(amount)

    def named(tallies, offset_by):
        used = int((tallies > 0).sum())
        fixed = max(1, used // 4)
        moved = fixed + (places - fixed + offset_by * (used - fixed)) % max(1, amount - fixed)
        return jnp.zeros((amount,), jnp.int32).at[sequence[jnp.where(places < fixed, places, moved)]].set(jnp.asarray(tallies, jnp.int32))

    tallies = jnp.where(number % 4 == 0, named(packed, number // 4), named(common, number - number // 4 - 1))
    mixed = jax.random.permutation(jax.random.fold_in(own, 3), amount)
    source_of, sink = mixed[0:amount // 2 * 2:2], mixed[1:amount // 2 * 2:2]
    slack = jnp.minimum(tallies[source_of] - 1, reach - tallies[sink]) // 2
    slack = jnp.where((source_of == sequence[0]) | (sink == sequence[0]) | (tallies[sink] == 0), 0, jnp.maximum(slack, 0))
    moved = jax.random.randint(jax.random.fold_in(own, 4), (amount // 2,), 0, 1 << 20) % (slack + 1)
    tallies = tallies.at[source_of].add(-moved).at[sink].add(moved)
    labels = jnp.searchsorted(jnp.cumsum(tallies), jnp.arange(rows * top), side="right").astype(jnp.int32)
    grid = labels.reshape(top, rows).T
    grid = grid[jax.random.permutation(jax.random.fold_in(own, 1), rows)]
    offset_by = jax.random.randint(jax.random.fold_in(own, 2), (rows, 1), 0, top)
    return jnp.take_along_axis(grid, (jnp.arange(top)[None, :] + offset_by) % top, axis=1)


def portions_of(amount, total, bound, slope, full):
    portions = [(1 << 20) // math.isqrt(grade ** slope) + 1 for grade in range(1, amount + 1)]
    largest = bound if full else min(bound, max(-(-total // amount), total * portions[0] // sum(portions)))
    least = 1 if total - largest >= amount - 1 else 0
    holding, rest = [largest] + [least] * (amount - 1), total - largest - least * (amount - 1)
    while rest > 0:
        movable = [i for i in range(1, amount) if holding[i] < largest] or [i for i in range(1, amount) if holding[i] < bound]
        mass, remaining = sum([portions[i] for i in movable]), rest
        for i in movable:
            addition = min(bound - holding[i], max(1, remaining * portions[i] // mass), rest)
            holding[i] = holding[i] + addition
            rest = rest - addition
    return np.array(holding)


def gaussian(own_key, dims, spread, bound, cuts=(), held_as=jnp.bfloat16):
    entries = spread * jax.random.normal(own_key, dims, jnp.float32)
    if cuts:
        entries = entries * level_of(own_key, dims, cuts, -0.22, 0.18)
    return jnp.clip(entries, -bound, bound).astype(held_as)


def setup_inputs(seed: int = 0) -> dict:
    streams_of = jax.random.split(jax.random.key(seed), 9)
    patch_qkv = draw_patch_qkv(jax.random.fold_in(streams_of[8], 71), 0)
    patch_state = gaussian(streams_of[1], (PATCHES, HV), 1.0, 6.0, ((0, 512),))
    window_index = jax.vmap(lambda own: jax.random.permutation(own, P_DEV))(jax.random.split(streams_of[2], (N_SEC * N_SP * N_DEV))).reshape((N_SEC * N_SP * N_DEV, P_DEV)).astype(jnp.int32)
    patch_owner_keys = jax.random.split(jax.random.fold_in(streams_of[3], 1), PATCHES // P_DEV)
    patch_owner_turns = jax.random.permutation(jax.random.fold_in(streams_of[3], 3), PATCHES // P_DEV)
    patch_owner = jax.vmap(lambda own, number: shared_out(jax.random.fold_in(streams_of[3], 2), own, number, P_DEV, OWNERS, 1, CAP, 2))(patch_owner_keys, patch_owner_turns).reshape((PATCHES, 1))
    source_request = jax.vmap(lambda own: jnp.searchsorted(jnp.cumsum(ragged_sizes(own, REQS, OWNERS, RMOST, 2)), jnp.arange(OWNERS), side="right"))(jax.random.split(streams_of[4], OWNERS)).reshape((OWNERS, OWNERS)).astype(jnp.int32)
    norm_gain = jnp.clip(1.0 + 0.18 * jax.random.normal(streams_of[5], (HV,), jnp.float32), 0.1, 1.9)
    w_qkv = gaussian(streams_of[6], (HV, 3, HV), HV ** -0.5, 0.15625, ((2, 4),))
    b_qkv = draw_b_qkv(jax.random.fold_in(streams_of[8], 71), 0)
    return dict(patch_qkv=patch_qkv, patch_state=patch_state, window_index=window_index, patch_owner=patch_owner, source_request=source_request, norm_gain=norm_gain, w_qkv=w_qkv, b_qkv=b_qkv)


NORM_EPS = 1e-06

def normalize(rows_in, gain_row):
    rows_in = rows_in.astype(jnp.float32)
    mean_sq = lax.optimization_barrier(jnp.mean(rows_in * rows_in, axis=-1, keepdims=True))
    return (rows_in * lax.rsqrt(mean_sq + NORM_EPS) * gain_row).astype(jnp.bfloat16)

def softmax_rows(scores):
    row_max = lax.optimization_barrier(jnp.max(scores, axis=-1, keepdims=True))
    expo_vals = jnp.exp(scores - row_max)
    return (expo_vals / lax.optimization_barrier(jnp.sum(expo_vals, axis=-1, keepdims=True))).astype(jnp.bfloat16)

def window_attend(qkv_rows, order_ids, head_count, head_size, window_span):
    num_rows = qkv_rows.shape[0]
    row_width = head_count * head_size
    ordered = jnp.take(qkv_rows, order_ids, axis=0).astype(jnp.float32)
    ordered = ordered.reshape(num_rows // window_span, window_span, 3, head_count, head_size)
    scores = jnp.einsum('wqhd,wkhd->whqk', ordered[:, :, 0], ordered[:, :, 1]) * head_size ** (-0.5)
    weights = softmax_rows(scores)
    weights = lax.optimization_barrier(weights).astype(jnp.float32)
    mixed = jnp.einsum('whqk,wkhd->wqhd', weights, ordered[:, :, 2])
    mixed = mixed.reshape(num_rows, row_width).astype(jnp.bfloat16)
    return jnp.zeros((num_rows, row_width), jnp.bfloat16).at[order_ids].set(mixed)

def owner_attend(group_rows, live_slots, request, gain_row, w_all, b_all, head_count, head_size):
    group_size = group_rows.shape[0]
    normed = normalize(group_rows, gain_row)
    projected = jnp.dot(normed, w_all.reshape(w_all.shape[0], -1), preferred_element_type=jnp.float32)
    projected = projected.reshape(group_size, 3, -1) + b_all.astype(jnp.float32)
    projected = lax.optimization_barrier(projected.astype(jnp.bfloat16)).astype(jnp.float32)
    projected = projected.reshape(group_size, 3, head_count, head_size)
    scores = jnp.einsum('qhd,khd->hqk', projected[:, 0], projected[:, 1])
    allowed = (request[:, None] == request[None, :]) & (live_slots[None, :] > 0)
    scores = jnp.where(allowed[None], scores * head_size ** (-0.5), -1e+30)
    weights = lax.optimization_barrier(softmax_rows(scores)).astype(jnp.float32)
    mixed = jnp.einsum('hqk,khd->qhd', weights, projected[:, 2])
    return mixed.reshape(group_size, head_count * head_size).astype(jnp.bfloat16)

def reference(patch_qkv, patch_state, window_index, patch_owner, source_request, norm_gain, w_qkv, b_qkv):
    devices = N_SEC * N_SP * N_DEV
    owners = N_SEC * N_DEV
    qkv_dev = patch_qkv.reshape(devices, P_DEV, 3, HV)
    window_out = lax.map(lambda key_item: window_attend(key_item[0], key_item[1], HEADS, HD, WIN), (qkv_dev, window_index))
    window_out = lax.optimization_barrier(window_out)
    state_rows = patch_state.reshape(devices, P_DEV, HV)
    moved = (state_rows.astype(jnp.float32) + window_out.astype(jnp.float32)).astype(jnp.bfloat16)
    owner_id = patch_owner.reshape(devices, P_DEV).astype(jnp.int32)
    owner_hits = (owner_id[:, :, None] == jnp.arange(owners, dtype=jnp.int32)[None, None, :]).astype(jnp.int32)
    slot_rank = lax.optimization_barrier(jnp.sum((jnp.cumsum(owner_hits, axis=1) - 1) * owner_hits, axis=2)).astype(jnp.int32)
    slot_id = (owner_id * CAP + slot_rank).astype(jnp.int32)
    row_ids = jnp.arange(devices, dtype=jnp.int32)[:, None]
    buffer = jnp.zeros((devices, owners * CAP, HV), jnp.bfloat16).at[row_ids, slot_id].set(moved)
    live_slots = jnp.zeros((devices, owners * CAP), jnp.int32).at[row_ids, slot_id].set(1)
    grouped = buffer.reshape(N_SEC, N_SP, N_DEV, owners, CAP, HV).transpose(3, 0, 2, 1, 4, 5).reshape(owners, -1, HV)
    live_group = live_slots.reshape(N_SEC, N_SP, N_DEV, owners, CAP).transpose(3, 0, 2, 1, 4).reshape(owners, -1)
    request = jnp.repeat(source_request, N_SP * CAP, axis=1)
    mixed = lax.map(lambda key_item: owner_attend(key_item[0], key_item[1], key_item[2], norm_gain, w_qkv, b_qkv, HEADS, HD), (grouped, live_group, request))
    back_rows = mixed.reshape(owners, N_SEC, N_DEV, N_SP, CAP, HV).transpose(1, 3, 2, 0, 4, 5).reshape(devices, owners * CAP, HV)
    gathered = jnp.take_along_axis(back_rows, slot_id[:, :, None], axis=1)
    result = (moved.astype(jnp.float32) + gathered.astype(jnp.float32)).astype(jnp.bfloat16)
    return result.reshape(devices * P_DEV, HV)
```

```python
import jax
import jax.numpy as jnp
from jax import lax
from jax.sharding import PartitionSpec as P

HD = 80
WIN = 64


NORM_EPS = 1e-06


def normalize(rows_in, gain_row):
    rows_in = rows_in.astype(jnp.float32)
    mean_sq = jnp.mean(rows_in * rows_in, axis=-1, keepdims=True)
    return (rows_in * lax.rsqrt(mean_sq + NORM_EPS) * gain_row).astype(jnp.bfloat16)


def softmax_rows(scores):
    row_max = jnp.max(scores, axis=-1, keepdims=True)
    expo_vals = jnp.exp(scores - row_max)
    return (expo_vals / jnp.sum(expo_vals, axis=-1, keepdims=True)).astype(jnp.bfloat16)


def window_attend(qkv_rows, order_ids, head_size, window_span):
    num_rows = qkv_rows.shape[0]
    row_width = qkv_rows.shape[2]
    head_count = row_width // head_size
    ordered = jnp.take(qkv_rows, order_ids, axis=0)
    ordered = ordered.reshape(num_rows // window_span, window_span, 3, head_count, head_size)
    scores = jnp.einsum(
        "wqhd,wkhd->whqk", ordered[:, :, 0], ordered[:, :, 1], preferred_element_type=jnp.float32
    ) * head_size ** (-0.5)
    weights = softmax_rows(scores)
    mixed = jnp.einsum(
        "whqk,wkhd->wqhd", weights, ordered[:, :, 2], preferred_element_type=jnp.float32
    )
    mixed = mixed.reshape(num_rows, row_width).astype(jnp.bfloat16)
    return jnp.zeros((num_rows, row_width), jnp.bfloat16).at[order_ids].set(mixed)


def owner_attend(query, keys_all, values_all, request, live_keys, head_size):
    group_size, head_count, _ = query.shape
    q_block = 512
    scale = head_size ** (-0.5)
    open_keys = live_keys > 0

    def one_block(block_start):
        rows_q = lax.dynamic_slice_in_dim(query, block_start, q_block, 0)
        reqs_q = lax.dynamic_slice_in_dim(request, block_start, q_block, 0)
        scores = jnp.einsum("qhd,khd->hqk", rows_q, keys_all, preferred_element_type=jnp.float32)
        allowed = (reqs_q[:, None] == request[None, :]) & open_keys[None, :]
        scores = jnp.where(allowed[None], scores * scale, -1e30)
        weights = softmax_rows(scores)
        mixed = jnp.einsum("hqk,khd->qhd", weights, values_all, preferred_element_type=jnp.float32)
        return mixed.astype(jnp.bfloat16)

    starts = jnp.arange(group_size // q_block, dtype=jnp.int32) * q_block
    blocks = lax.map(one_block, starts)
    return blocks.reshape(group_size, head_count * head_size)


def shards(
    patch_qkv, patch_state, window_index, patch_owner, source_request, norm_gain, w_qkv, b_qkv
):
    num_rows = patch_qkv.shape[0]
    row_width = patch_qkv.shape[2]
    sections = lax.axis_size("sec")
    groups = lax.axis_size("sp")
    members = lax.axis_size("dev")
    owners = sections * members
    capacity = max(2, 2 * num_rows // owners)
    local_width = w_qkv.shape[2]
    local_heads = local_width // HD
    window_out = lax.optimization_barrier(window_attend(patch_qkv, window_index[0], HD, WIN))
    moved = (patch_state.astype(jnp.float32) + window_out.astype(jnp.float32)).astype(jnp.bfloat16)
    owner_id = patch_owner[:, 0]
    position = jnp.arange(num_rows, dtype=jnp.int32)
    earlier = (owner_id[:, None] == owner_id[None, :]) & (position[None, :] < position[:, None])
    slot_rank = jnp.sum(earlier.astype(jnp.int32), axis=1)
    slot_id = owner_id * capacity + slot_rank
    picker = (jnp.arange(owners * capacity, dtype=jnp.int32)[:, None] == slot_id[None, :]).astype(
        jnp.bfloat16
    )
    outgoing = jnp.dot(picker, moved, preferred_element_type=jnp.float32).astype(jnp.bfloat16)
    outgoing = outgoing.reshape(owners, capacity, row_width)
    filled = jnp.max(picker, axis=1).reshape(owners, capacity)
    incoming, arrived = (
        lax.all_to_all(outgoing, ("sec", "dev"), split_axis=0, concat_axis=0, tiled=True),
        lax.all_to_all(filled, ("sec", "dev"), split_axis=0, concat_axis=0, tiled=True),
    )
    group_size = owners * groups * capacity
    rows_all, live_all = (
        lax.all_gather(incoming, "sp", axis=1, tiled=True),
        lax.all_gather(arrived, "sp", axis=1, tiled=True),
    )
    normed = normalize(rows_all.reshape(group_size, row_width), norm_gain)
    projected = jnp.einsum("gf,fch->gch", normed, w_qkv, preferred_element_type=jnp.float32)
    projected = (projected + b_qkv.astype(jnp.float32)).astype(jnp.bfloat16)
    query = projected[:, 0].reshape(group_size, local_heads, HD)
    keys_all = projected[:, 1].reshape(group_size, local_heads, HD)
    values_all = projected[:, 2].reshape(group_size, local_heads, HD)
    request = jnp.repeat(source_request[0], groups * capacity)
    live_keys = live_all.reshape(group_size)
    mixed = owner_attend(query, keys_all, values_all, request, live_keys, HD)
    pieces = mixed.reshape(owners, groups, capacity, local_width)
    returned = lax.all_to_all(pieces, "sp", split_axis=1, concat_axis=3, tiled=True).reshape(
        owners, capacity, row_width
    )
    result = lax.all_to_all(returned, ("sec", "dev"), split_axis=0, concat_axis=0, tiled=True)
    result = result.reshape(owners * capacity, row_width)
    back_rows = jnp.einsum("sp,sw->pw", picker, result, preferred_element_type=jnp.float32)
    return (moved.astype(jnp.float32) + back_rows).astype(jnp.bfloat16)


def solution(mesh):
    in_specs = (
        P(("sec", "sp", "dev"), None, None),
        P(("sec", "sp", "dev"), None),
        P(("sec", "sp", "dev"), None),
        P(("sec", "sp", "dev"), None),
        P(("sec", "dev"), None),
        P(),
        P(None, None, "sp"),
        P(None, "sp"),
    )
    out_specs = P(("sec", "sp", "dev"), None)
    return jax.shard_map(shards, mesh=mesh, in_specs=in_specs, out_specs=out_specs, check_vma=False)
```

```python
import functools

import jax
import jax.numpy as jnp
from jax import lax
from jax.experimental import pallas as pl
from jax.experimental.pallas import tpu as pltpu
from jax.sharding import PartitionSpec as P

HD = 80
NORM_EPS = 1e-06
NZ, NX, NC, NY = 16, 4, 2, 4
NP = NX * NC
ROWS, WIDTH = 128, 1280
LANES = 128
HEADS_HERE = 4
PART = HEADS_HERE * LANES
PAIR = 2 * HEADS_HERE * HD
DEAD = 1024.0
SCALE = HD ** (-0.5)
LOG2E = 1.4426950408889634
MESH = pl.DeviceIdType.MESH
BF, F32, I32 = jnp.bfloat16, jnp.float32, jnp.int32


def hop(i):
    return (8 + (2 * (i % 2) - 1) * ((i + 1) // 2)) % NZ


def hop_of(i):
    return (8 + (2 * (i & 1) - 1) * ((i + 1) >> 1)) & (NZ - 1)


def iota(shape, axis):
    return lax.broadcasted_iota(I32, shape, axis)


def dot(a, b):
    return jnp.dot(a, b, preferred_element_type=F32)


def dot_nt(a, b):
    return lax.dot_general(a, b, (((1,), (1,)), ((), ())), preferred_element_type=F32)


def onehot(mask):
    return jnp.where(mask, 1.0, 0.0).astype(BF)


def rows16(index):
    return pl.ds(pl.multiple_of(index * 16, 16), 16)


def kernel(
    qkv_ref, state_ref, order_ref, owner_ref, request_ref, gain_ref, w_hbm, bias_ref, out_ref,
    moved, outgoing, plane_in, z_out, group, w_ref, asks, queries, keys, values, mixed,
    pieces, plane_back, z_back, final,
    w_sem, p_send, p_recv, z_send, z_recv, y_send, yl_recv, yr_recv, yx_recv,
    b_send, b_recv, r_send, r_recv,
):
    sec, sp, dev = (lax.axis_index(a) for a in ("sec", "sp", "dev"))
    x, z = dev // NZ, dev % NZ
    cx = sec * NX + x
    right, left = (sp + 1) % NY, (sp + 3) % NY

    load_w = pltpu.make_async_copy(w_hbm, w_ref, w_sem)
    load_w.start()

    def plane_id(to_cx, to_y):
        return (to_cx // NX, to_y, (to_cx % NX) * NZ + z)

    def z_id(to_z):
        return (sec, sp, x * NZ + to_z)

    barrier = pltpu.get_barrier_semaphore()

    def greet_plane(k, carry):
        pl.semaphore_signal(
            barrier, inc=1, device_id=plane_id((cx + k // NY) % NP, (sp + k % NY) % NY), device_id_type=MESH
        )
        return carry

    def greet_z(k, carry):
        pl.semaphore_signal(barrier, inc=1, device_id=z_id((z + k) % NZ), device_id_type=MESH)
        return carry

    lax.fori_loop(1, NP * NY, greet_plane, 0)
    lax.fori_loop(1, NZ, greet_z, 0)

    owner_cols = jnp.broadcast_to(owner_ref[...].astype(F32), (ROWS, ROWS))
    owner_rows = jnp.transpose(owner_cols)
    row_i, col_i = iota((ROWS, ROWS), 0), iota((ROWS, ROWS), 1)
    same = owner_cols == owner_rows
    rank_row = jnp.sum(jnp.where(same & (row_i < col_i), 1.0, 0.0), axis=0, keepdims=True)
    rank_col = jnp.sum(jnp.where(same & (col_i < row_i), 1.0, 0.0), axis=1, keepdims=True)

    order = jnp.broadcast_to(order_ref[...], (ROWS, ROWS))
    in_second = jnp.sum(jnp.where((order == row_i) & (col_i >= 64), 1.0, 0.0), axis=1, keepdims=True)
    second_cols = jnp.broadcast_to(in_second, (ROWS, ROWS))
    same_window = second_cols == jnp.transpose(second_cols)

    def window_half(half, carry):
        base = half * 640
        tiles = [jnp.zeros((ROWS, LANES), F32) for _ in range(5)]
        for head in range(8):
            low, high = head * HD, head * HD + HD
            first, last = low // LANES, (high + LANES - 1) // LANES
            span = (last - first) * LANES
            columns = pl.ds(pl.multiple_of(base + first * LANES, LANES), span)
            lane = iota((ROWS, span), 1) + first * LANES
            mine = (lane >= low) & (lane < high)
            q = qkv_ref[0, :, columns]
            q = jnp.where(mine, q.astype(F32), 0.0).astype(BF)
            scores = dot_nt(q, qkv_ref[1, :, columns])
            scores = jnp.where(same_window, scores * SCALE, -1e30)
            top = jnp.max(scores, axis=1, keepdims=True)
            expo = jnp.exp(scores - top)
            weights = (expo / jnp.sum(expo, axis=1, keepdims=True)).astype(BF)
            got = dot(weights, qkv_ref[2, :, columns])
            got = jnp.where(mine, got, 0.0)
            for t in range(first, last):
                tiles[t] = tiles[t] + got[:, (t - first) * LANES : (t - first + 1) * LANES]
        for t in range(5):
            columns = pl.ds(pl.multiple_of(base + t * LANES, LANES), LANES)
            window_out = tiles[t].astype(BF).astype(F32)
            moved[:, columns] = (state_ref[:, columns].astype(F32) + window_out).astype(BF)
        return carry

    lax.fori_loop(0, 2, window_half, 0)

    slot_i = iota((256, ROWS), 0)
    index = ((slot_i >> 7) << 3) + ((slot_i >> 1) & 7)
    to_owner = ((slot_i >> 4) & 7) * NZ + ((z + hop_of(index)) & (NZ - 1))
    chosen = (owner_rows[0:1] == to_owner.astype(F32)) & (rank_row == (slot_i & 1).astype(F32))
    picker = onehot(chosen)
    taken = jnp.max(jnp.where(chosen, 1.0, 0.0), axis=1, keepdims=True)
    outgoing[:, 0:LANES] = jnp.where(taken > 0.5, dot(picker, moved[:, 0:LANES]), DEAD).astype(BF)
    outgoing[:, LANES:] = dot(picker, moved[:, LANES:]).astype(BF)

    pl.semaphore_wait(barrier, NP * NY - 1 + NZ - 1)

    for half in range(2):

        def send_plane(k, carry):
            to = (cx + k) % NP
            pltpu.make_async_remote_copy(
                src_ref=outgoing.at[rows16(half * NP + to)], dst_ref=plane_in.at[rows16(half * NP + cx)],
                send_sem=p_send, recv_sem=p_recv.at[half], device_id=plane_id(to, sp), device_id_type=MESH,
            ).start()
            return carry

        lax.fori_loop(1, NP, send_plane, 0)
        plane_in[rows16(half * NP + cx)] = outgoing[rows16(half * NP + cx)]

    def local(ref, rows, send_sem, recv_sem):
        part = ref.at[pl.ds(0, rows)]
        return pltpu.make_async_remote_copy(
            src_ref=part, dst_ref=part, send_sem=send_sem, recv_sem=recv_sem,
            device_id=(sec, right, dev), device_id_type=MESH,
        )

    r, c = iota((ROWS, ROWS), 0), iota((ROWS, ROWS), 1)
    by_hop = onehot(c == (r & 7) * 16 + (r >> 4) * 2 + ((r >> 3) & 1))

    def send_z(i, carry):
        pltpu.make_async_remote_copy(
            src_ref=z_out.at[rows16(i)], dst_ref=group.at[rows16(i * NY + sp)],
            send_sem=z_send, recv_sem=z_recv.at[i], device_id=z_id((z + hop(i)) % NZ), device_id_type=MESH,
        ).start()
        return carry

    for half in range(2):
        local(plane_in, 7 * 16, p_send, p_recv.at[half]).wait_recv()
        z_out[half * 128 : half * 128 + 128] = dot(by_hop, plane_in[half * 128 : half * 128 + 128]).astype(BF)
        lax.fori_loop(half * 8, 8 if half == 0 else 15, send_z, 0)
    group[rows16(15 * NY + sp)] = z_out[240:256]

    r, c = iota((1024, LANES), 0), iota((1024, LANES), 1)
    source = (r & 7) * NZ + ((z - hop_of(r >> 6)) & (NZ - 1))
    lane_request = onehot(jnp.broadcast_to(request_ref[...], (LANES, LANES)) == row_i - HD)
    asks[...] = dot_nt(onehot(c == source), lane_request).astype(BF)
    load_w.wait()

    r, c = iota((256, 256), 0), iota((256, 256), 1)
    by_source = onehot(c == (r & 3) * 64 + ((r >> 2) & 3) * 16 + ((r >> 4) & 1) * 8 + (r >> 5))

    def send_y(i, from_y, to_y, recv_sem):
        part = group.at[rows16(i * NY + from_y)]
        pltpu.make_async_remote_copy(
            src_ref=part, dst_ref=part, send_sem=y_send, recv_sem=recv_sem,
            device_id=(sec, to_y, dev), device_id_type=MESH,
        ).start()

    def wait_one(recv_sem):
        local(group, 16, y_send, recv_sem).wait_recv()

    def relay(i):
        if i % 2 == 0:
            wait_one(yl_recv.at[i])
            send_y(i, left, right, yx_recv.at[i])
        else:
            wait_one(yr_recv.at[i])
            send_y(i, right, left, yx_recv.at[i])

    def project(k):
        for i in range(4 * k, 4 * k + 4):
            wait_one(yr_recv.at[i] if i % 2 == 0 else yl_recv.at[i])
            wait_one(yx_recv.at[i])
        rows = slice(256 * k, 256 * k + 256)
        raw = group[rows].astype(F32)
        live = raw[:, 0:1] < DEAD / 2
        mean_sq = jnp.mean(raw * raw, axis=1, keepdims=True)
        normed = (raw * lax.rsqrt(mean_sq + NORM_EPS) * gain_ref[...]).astype(BF)
        ask = asks[rows].astype(F32)
        lane = iota((256, LANES), 1)
        shut = jnp.where((lane >= HD) & (lane < HD + 8) & ~((ask > 0.5) & live), -1e30, 0.0)
        ones = jnp.where(lane == HD, 1.0, 0.0)
        for part, extra in enumerate((ask, shut, ones)):
            extra = jnp.concatenate([extra, extra], axis=1)
            for pair in range(2):
                columns = slice(part * PART + pair * 256, part * PART + pair * 256 + 256)
                here = slice(pair * 256, pair * 256 + 256)
                got = (dot(normed, w_ref[:, columns]) + (bias_ref[:, columns] + extra)).astype(BF)
                if part == 0:
                    got = dot(by_source, got).astype(BF)
                    for n in range(NP):
                        queries[n * 128 + k * 32 : n * 128 + k * 32 + 32, here] = got[n * 32 : n * 32 + 32]
                elif part == 1:
                    keys[rows, here] = got
                else:
                    values[rows, here] = got

    for i in range(16):
        if i < 15:
            local(group, 16, z_send, z_recv.at[i]).wait_recv()
        send_y(i, sp, right, yl_recv.at[i])
        send_y(i, sp, left, yr_recv.at[i])
        if i >= 1:
            relay(i - 1)
        if i >= 6 and i % 4 == 2:
            project(i // 4 - 1)
    relay(15)
    project(3)

    r, c = iota((PART, PAIR), 0), iota((PART, PAIR), 1)
    spot = (r >> 7) * HD + (r & 127)
    real = (r & 127) < HD
    place = [onehot(real & (c == spot + slot * HEADS_HERE * HD)) for slot in range(2)]
    r, c = iota((64, 256), 0), iota((64, 256), 1)
    gather_slots = onehot((c & 127) == ((r >> 2) & 3) * 32 + (c >> 7) * 16 + (r >> 4) * 4 + (r & 3))

    def attend(t):
        blocks = [pl.ds(pl.multiple_of(((cx + 2 * t + n) % NP) * 128, 128), 128) for n in range(2)]
        for head in range(HEADS_HERE):
            here = slice(head * LANES, head * LANES + LANES)
            q = jnp.concatenate([queries[b, here] for b in blocks], axis=0)
            scores = dot_nt(q, keys[:, here])
            top = jnp.max(scores, axis=1, keepdims=True)
            weights = jnp.exp2((scores - top) * (SCALE * LOG2E)).astype(BF)
            got = dot(weights, values[:, here])
            mixed[:, here] = (got / got[:, HD : HD + 1]).astype(BF)
        placed = [dot(mixed[...], p).astype(BF) for p in place]
        for n in range(2):
            e = 2 * t + n
            both = jnp.concatenate([p[n * 128 : n * 128 + 128] for p in placed], axis=0)
            pieces[e * 64 : e * 64 + 64] = dot(gather_slots, both).astype(BF)
            to = (cx + e) % NP
            for dy in range(NY):
                y = (sp + dy) % NY
                if e == 0 and dy == 0:
                    plane_back[rows16(sp)] = pieces[rows16(sp)]
                    continue
                pltpu.make_async_remote_copy(
                    src_ref=pieces.at[rows16(e * NY + y)], dst_ref=plane_back.at[rows16(e * NY + sp)],
                    send_sem=b_send, recv_sem=b_recv.at[e // 4], device_id=plane_id(to, y), device_id_type=MESH,
                ).start()

    r, c = iota((256, 256), 0), iota((256, 256), 1)
    by_hop_back = onehot(c == (r & 15) * 16 + (r >> 4))

    def give_back(half):
        local(plane_back, (15 + half) * 16, b_send, b_recv.at[half]).wait_recv()
        z_back[half * 256 : half * 256 + 256] = dot(by_hop_back, plane_back[half * 256 : half * 256 + 256]).astype(BF)

        def send_back(i, carry):
            rows = rows16(half * 16 + i)
            pltpu.make_async_remote_copy(
                src_ref=z_back.at[rows], dst_ref=final.at[rows], send_sem=r_send, recv_sem=r_recv,
                device_id=z_id((z + NZ - hop(i)) % NZ), device_id_type=MESH,
            ).start()
            return carry

        lax.fori_loop(0, 15, send_back, 0)
        final[half * 256 + 240 : half * 256 + 256] = z_back[half * 256 + 240 : half * 256 + 256]

    attend(0)
    attend(1)
    attend(2)
    give_back(0)
    attend(3)
    give_back(1)

    f = iota((1, 512), 1)
    from_cx = (cx - ((f >> 8) * 4 + ((f >> 2) & 3))) & (NP - 1)
    from_owner = (from_cx * NZ + ((z + hop_of((f >> 4) & 15)) & (NZ - 1))).astype(F32)
    mine = jnp.where(owner_cols[:, 0:1] == from_owner, 1.0, 0.0)
    local(final, 480, r_send, r_recv).wait_recv()
    lane = iota((ROWS, PAIR), 1)
    for pair in range(2):
        found = []
        for n in range(2):
            pick = jnp.where((f & 3) == 2 * pair + n, mine, 0.0).astype(BF)
            got = dot(pick, final[...])
            turned = pltpu.roll(got, PAIR // 2, 1)
            found.append(jnp.where(rank_col == float(n), got, turned))
        back = jnp.where(lane < PAIR // 2, found[0], found[1])
        columns = slice(pair * PAIR, pair * PAIR + PAIR)
        out_ref[:, columns] = (moved[:, columns].astype(F32) + back).astype(BF)

    local(outgoing, 14 * 16, p_send, p_recv.at[0]).wait_send()
    local(z_out, 15 * 16, z_send, z_recv.at[0]).wait_send()
    local(group, 48 * 16, y_send, yx_recv.at[0]).wait_send()
    local(pieces, 31 * 16, b_send, b_recv.at[0]).wait_send()
    local(z_back, 30 * 16, r_send, r_recv).wait_send()


def shards(
    patch_qkv, patch_state, window_index, patch_owner, source_request, norm_gain, w_qkv, b_qkv
):
    qkv = jnp.transpose(patch_qkv, (1, 0, 2))
    w = w_qkv.reshape(WIDTH, 3 * HEADS_HERE, HD)
    w = jnp.pad(w, ((0, 0), (0, 0), (0, LANES - HD))).reshape(WIDTH, 3 * PART)
    bias = jnp.pad(b_qkv.astype(F32).reshape(3 * HEADS_HERE, HD), ((0, 0), (0, LANES - HD))).reshape(1, 3 * PART)
    vmem = pl.BlockSpec(memory_space=pltpu.VMEM)
    dma = pltpu.SemaphoreType.DMA
    return pl.pallas_call(
        kernel,
        out_shape=jax.ShapeDtypeStruct((ROWS, WIDTH), BF),
        in_specs=[vmem] * 6 + [pl.BlockSpec(memory_space=pl.ANY), vmem],
        out_specs=vmem,
        scratch_shapes=[
            pltpu.VMEM((ROWS, WIDTH), BF),
            pltpu.VMEM((256, WIDTH), BF),
            pltpu.VMEM((256, WIDTH), BF),
            pltpu.VMEM((256, WIDTH), BF),
            pltpu.VMEM((1024, WIDTH), BF),
            pltpu.VMEM((WIDTH, 3 * PART), BF),
            pltpu.VMEM((1024, LANES), BF),
            pltpu.VMEM((1024, PART), BF),
            pltpu.VMEM((1024, PART), BF),
            pltpu.VMEM((1024, PART), BF),
            pltpu.VMEM((256, PART), BF),
            pltpu.VMEM((512, PAIR), BF),
            pltpu.VMEM((512, PAIR), BF),
            pltpu.VMEM((512, PAIR), BF),
            pltpu.VMEM((512, PAIR), BF),
            dma, dma, dma((2,)), dma, dma((16,)), dma, dma((16,)), dma((16,)), dma((16,)),
            dma, dma((2,)), dma, dma,
        ],
        compiler_params=pltpu.CompilerParams(
            collective_id=0, has_side_effects=True, vmem_limit_bytes=48 * 1024 * 1024
        ),
    )(qkv, patch_state, window_index, patch_owner, source_request, norm_gain.reshape(1, WIDTH), w, bias)


def solution(mesh):
    in_specs = (
        P(("sec", "sp", "dev"), None, None),
        P(("sec", "sp", "dev"), None),
        P(("sec", "sp", "dev"), None),
        P(("sec", "sp", "dev"), None),
        P(("sec", "dev"), None),
        P(),
        P(None, None, "sp"),
        P(None, "sp"),
    )
    out_specs = P(("sec", "sp", "dev"), None)
    return jax.shard_map(shards, mesh=mesh, in_specs=in_specs, out_specs=out_specs, check_vma=False)
```

```python
import functools

import jax
import jax.numpy as jnp
from jax import lax
from jax.experimental import pallas as pl
from jax.experimental.pallas import tpu as pltpu
from jax.sharding import PartitionSpec as P

HD = 80
NORM_EPS = 1e-06
NZ, NX, NC, NY = 16, 4, 2, 4
NP = NX * NC
ROWS, WIDTH = 128, 1280
LANES = 128
HEADS_HERE = 4
PART = HEADS_HERE * LANES
PAIR = 2 * HEADS_HERE * HD
DEAD = 1024.0
SCALE = HD ** (-0.5)
LOG2E = 1.4426950408889634
MESH = pl.DeviceIdType.MESH
BF, F32, I32 = jnp.bfloat16, jnp.float32, jnp.int32


def hop(i):
    return ((2 * (i % 2) - 1) * ((i + 1) // 2)) % NZ


def hop_of(i):
    return ((2 * (i & 1) - 1) * ((i + 1) >> 1)) & (NZ - 1)


def iota(shape, axis):
    return lax.broadcasted_iota(I32, shape, axis)


def dot(a, b):
    return jnp.dot(a, b, preferred_element_type=F32)


def dot_nt(a, b):
    return lax.dot_general(a, b, (((1,), (1,)), ((), ())), preferred_element_type=F32)


def onehot(mask):
    return jnp.where(mask, 1.0, 0.0).astype(BF)


def rows16(index):
    return pl.ds(pl.multiple_of(index * 16, 16), 16)


def kernel(
    qkv_hbm, state_hbm, order_ref, owner_ref, request_ref, gain_ref, w_hbm, b_ref, out_ref,
    qkv_ref, state_ref, bias_ref,
    moved, outgoing, near_in, near_out, far_in, far_out, group, w_ref, asks, queries, keys, values, mixed,
    pieces, plane_back, z_back, back_in, back_out, final,
    q_sem, w_sem, n_send, nz_recv, nx_recv, f_send, fx_recv, fz_recv, y_send, yl_recv, yr_recv, yx_recv,
    b_send, b_recv, fb_recv, r_send, r_recv, rb_recv,
):
    sec, sp, dev = (lax.axis_index(a) for a in ("sec", "sp", "dev"))
    x, z = dev // NZ, dev % NZ
    cx = sec * NX + x
    right, left = (sp + 1) % NY, (sp + 3) % NY

    load_qkv = pltpu.make_async_copy(qkv_hbm, qkv_ref, q_sem.at[0])
    load_state = pltpu.make_async_copy(state_hbm, state_ref, q_sem.at[1])
    load_w = [
        pltpu.make_async_copy(
            w_hbm.at[part, pl.ds(head * HD, HD)], w_ref.at[pl.ds(part * PART + head * LANES, HD)],
            w_sem.at[part * HEADS_HERE + head],
        )
        for part in range(3)
        for head in range(HEADS_HERE)
    ]
    load_qkv.start()
    load_state.start()
    for load in load_w:
        load.start()

    def plane_id(to_cx, to_y):
        return (to_cx // NX, to_y, (to_cx % NX) * NZ + z)

    def z_id(to_z):
        return (sec, sp, x * NZ + to_z)

    gain = gain_ref[...].reshape(1, WIDTH)
    barrier = pltpu.get_barrier_semaphore()

    def greet_plane(k, carry):
        pl.semaphore_signal(
            barrier, inc=1, device_id=plane_id((cx + k // NY) % NP, (sp + k % NY) % NY), device_id_type=MESH
        )
        return carry

    def greet_z(k, carry):
        pl.semaphore_signal(barrier, inc=1, device_id=z_id((z + k) % NZ), device_id_type=MESH)
        return carry

    lax.fori_loop(1, NP * NY, greet_plane, 0)
    lax.fori_loop(1, NZ, greet_z, 0)

    owner_rows = jnp.broadcast_to(owner_ref[...].astype(F32), (ROWS, ROWS))
    owner_cols = jnp.transpose(owner_rows)
    row_i, col_i = iota((ROWS, ROWS), 0), iota((ROWS, ROWS), 1)
    same = owner_cols == owner_rows
    rank_row = jnp.sum(jnp.where(same & (row_i < col_i), 1.0, 0.0), axis=0, keepdims=True)
    rank_col = jnp.sum(jnp.where(same & (col_i < row_i), 1.0, 0.0), axis=1, keepdims=True)

    order = jnp.broadcast_to(order_ref[...], (ROWS, ROWS))
    in_second = jnp.sum(jnp.where((order == row_i) & (col_i >= 64), 1.0, 0.0), axis=1, keepdims=True)
    second_cols = jnp.broadcast_to(in_second, (ROWS, ROWS))
    same_window = second_cols == jnp.transpose(second_cols)

    def window_half(half, carry):
        base = half * 640
        tiles = [jnp.zeros((ROWS, LANES), F32) for _ in range(5)]
        for head in range(8):
            low, high = head * HD, head * HD + HD
            first, last = low // LANES, (high + LANES - 1) // LANES
            span = (last - first) * LANES
            columns = pl.ds(pl.multiple_of(base + first * LANES, LANES), span)
            lane = iota((ROWS, span), 1) + first * LANES
            mine = (lane >= low) & (lane < high)
            q = qkv_ref[0, :, columns]
            q = jnp.where(mine, q.astype(F32), 0.0).astype(BF)
            scores = dot_nt(q, qkv_ref[1, :, columns])
            scores = jnp.where(same_window, scores * SCALE, -1e30)
            top = jnp.max(scores, axis=1, keepdims=True)
            expo = jnp.exp(scores - top)
            weights = (expo / jnp.sum(expo, axis=1, keepdims=True)).astype(BF)
            got = dot(weights, qkv_ref[2, :, columns])
            got = jnp.where(mine, got, 0.0)
            for t in range(first, last):
                tiles[t] = tiles[t] + got[:, (t - first) * LANES : (t - first + 1) * LANES]
        for t in range(5):
            columns = pl.ds(pl.multiple_of(base + t * LANES, LANES), LANES)
            window_out = tiles[t].astype(BF).astype(F32)
            moved[:, columns] = (state_ref[:, columns].astype(F32) + window_out).astype(BF)
        return carry

    load_qkv.wait()
    load_state.wait()
    lax.fori_loop(0, 2, window_half, 0)

    slot_i = iota((256, ROWS), 0)
    high, low = (slot_i >> 4) & 7, (slot_i >> 1) & 7
    far = slot_i >= 128
    to_z = (z + hop_of(jnp.where(far, 8 + low, high))) & (NZ - 1)
    to_owner = jnp.where(far, high, low) * NZ + to_z
    chosen = (owner_rows[0:1] == to_owner.astype(F32)) & (rank_row == (slot_i & 1).astype(F32))
    picker = onehot(chosen)
    taken = jnp.max(jnp.where(chosen, 1.0, 0.0), axis=1, keepdims=True)
    outgoing[:, 0:LANES] = jnp.where(taken > 0.5, dot(picker, moved[:, 0:LANES]), DEAD).astype(BF)
    outgoing[:, LANES:] = dot(picker, moved[:, LANES:]).astype(BF)

    pl.semaphore_wait(barrier, NP * NY - 1 + NZ - 1)

    def start(src, dst, send_sem, recv_sem, to):
        pltpu.make_async_remote_copy(
            src_ref=src, dst_ref=dst, send_sem=send_sem, recv_sem=recv_sem, device_id=to, device_id_type=MESH
        ).start()

    def waiter(ref, rows, send_sem, recv_sem):
        part = ref.at[pl.ds(0, rows)]
        return pltpu.make_async_remote_copy(
            src_ref=part, dst_ref=part, send_sem=send_sem, recv_sem=recv_sem,
            device_id=(sec, right, dev), device_id_type=MESH,
        )

    def near_z(i, carry):
        rows = rows16(i)
        start(outgoing.at[rows], near_in.at[rows], n_send.at[0], nz_recv, z_id((z + hop(i)) % NZ))
        return carry

    def far_plane(k, carry):
        to = (cx + k) % NP
        start(outgoing.at[rows16(8 + to)], far_in.at[rows16(cx)], f_send.at[0], fx_recv, plane_id(to, sp))
        return carry

    lax.fori_loop(1, NP, far_plane, 0)
    lax.fori_loop(1, 8, near_z, 0)
    far_in[rows16(cx)] = outgoing[rows16(8 + cx)]
    near_in[0:16] = outgoing[0:16]

    r, c = iota((ROWS, ROWS), 0), iota((ROWS, ROWS), 1)
    swap = onehot(c == (r & 7) * 16 + (r >> 4) * 2 + ((r >> 3) & 1))

    waiter(far_in, 7 * 16, f_send.at[0], fx_recv).wait_recv()
    far_out[...] = dot(swap, far_in[...]).astype(BF)

    def far_z(n, carry):
        to = z_id((z + hop(8 + n)) % NZ)
        start(far_out.at[rows16(n)], group.at[rows16(32 + n * NY + sp)], f_send.at[1], fz_recv.at[n], to)
        return carry

    lax.fori_loop(0, 8, far_z, 0)

    waiter(near_in, 7 * 16, n_send.at[0], nz_recv).wait_recv()
    near_out[...] = dot(swap, near_in[...]).astype(BF)

    def near_plane(k, carry):
        to = (cx + k) % NP
        start(near_out.at[rows16(to)], group.at[rows16(cx * NY + sp)], n_send.at[1], nx_recv.at[k], plane_id(to, sp))
        return carry

    lax.fori_loop(1, NP, near_plane, 0)
    group[rows16(cx * NY + sp)] = near_out[rows16(cx)]

    r, c = iota((1024, LANES), 0), iota((1024, LANES), 1)
    high, low = (r >> 6) & 7, r & 7
    source = jnp.where(r < 512, high, low) * NZ + ((z - hop_of(jnp.where(r < 512, low, 8 + high))) & (NZ - 1))
    lane_request = onehot(jnp.broadcast_to(request_ref[...], (LANES, LANES)) == row_i - HD)
    asks[...] = dot_nt(onehot(c == source), lane_request).astype(BF)
    r, c = iota((HEADS_HERE * HD, PART), 0), iota((HEADS_HERE * HD, PART), 1)
    spread = onehot(((c & 127) < HD) & (r == (c >> 7) * HD + (c & 127)))
    for part in range(3):
        bias_ref[:, part * PART : part * PART + PART] = dot(b_ref[part : part + 1], spread)
        for head in range(HEADS_HERE):
            unused = part * PART + head * LANES + HD
            w_ref[unused : unused + LANES - HD] = jnp.zeros((LANES - HD, WIDTH), BF)
    for load in load_w:
        load.wait()

    r, c = iota((256, 256), 0), iota((256, 256), 1)
    by_source = onehot(c == (r & 3) * 64 + ((r >> 2) & 3) * 16 + ((r >> 4) & 1) * 8 + (r >> 5))

    def block(n, y):
        return rows16(((cx + NP - n) % NP if n < 8 else n) * NY + y)

    def send_y(n, from_y, to_y, recv_sem):
        part = group.at[block(n, from_y)]
        start(part, part, y_send, recv_sem, (sec, to_y, dev))

    def wait_one(recv_sem):
        waiter(group, 16, y_send, recv_sem).wait_recv()

    def forward(n):
        if n > 0:
            wait_one(nx_recv.at[n] if n < 8 else fz_recv.at[n - 8])
        send_y(n, sp, right, yl_recv.at[n])
        send_y(n, sp, left, yr_recv.at[n])

    def relay(n):
        if n % 2 == 0:
            wait_one(yl_recv.at[n])
            send_y(n, left, right, yx_recv.at[n])
        else:
            wait_one(yr_recv.at[n])
            send_y(n, right, left, yx_recv.at[n])

    def settle(n):
        wait_one(yr_recv.at[n] if n % 2 == 0 else yl_recv.at[n])
        wait_one(yx_recv.at[n])

    def project(k):
        rows = slice(256 * k, 256 * k + 256)
        raw = group[rows].astype(F32)
        live = raw[:, 0:1] < DEAD / 2
        mean_sq = jnp.mean(raw * raw, axis=1, keepdims=True)
        normed = (raw * lax.rsqrt(mean_sq + NORM_EPS) * gain).astype(BF)
        ask = asks[rows].astype(F32)
        lane = iota((256, LANES), 1)
        shut = jnp.where((lane >= HD) & (lane < HD + 8) & ~((ask > 0.5) & live), -1e30, 0.0)
        ones = jnp.where(lane == HD, 1.0, 0.0)
        for part, extra in enumerate((ask, shut, ones)):
            extra = jnp.concatenate([extra, extra], axis=1)
            for pair in range(2):
                columns = slice(part * PART + pair * 256, part * PART + pair * 256 + 256)
                here = slice(pair * 256, pair * 256 + 256)
                got = (dot_nt(normed, w_ref[columns]) + (bias_ref[:, columns] + extra)).astype(BF)
                if part == 0:
                    if k < 2:
                        for n in range(4):
                            to = (4 * k + n) * 128
                            queries[to : to + 64, here] = got[n * 64 : n * 64 + 64]
                        continue
                    got = dot(by_source, got).astype(BF)
                    for n in range(NP):
                        to = n * 128 + k * 32
                        queries[to : to + 32, here] = got[n * 32 : n * 32 + 32]
                elif part == 1:
                    keys[rows, here] = got
                else:
                    values[rows, here] = got

    for n in range(16):
        forward(n)
        if n >= 2:
            relay(n - 2)
        if n == 10:
            for m in range(8):
                settle(m)
            project(0)
        if n == 11:
            project(1)
        if n == 14:
            for m in range(8, 12):
                settle(m)
            project(2)
    relay(14)
    relay(15)
    for m in range(12, 16):
        settle(m)
    project(3)

    r, c = iota((PART, PAIR), 0), iota((PART, PAIR), 1)
    spot = (r >> 7) * HD + (r & 127)
    real = (r & 127) < HD
    place = [onehot(real & (c == spot + slot * HEADS_HERE * HD)) for slot in range(2)]
    r, c = iota((64, 256), 0), iota((64, 256), 1)
    slot, y, i = c >> 7, r >> 4, r & 15
    near_row, far_row = y * 16 + slot * 8 + i, 64 + ((i - 8) >> 2) * 32 + slot * 16 + y * 4 + (i & 3)
    gather_slots = onehot((c & 127) == jnp.where(i < 8, near_row, far_row))

    def attend(t):
        blocks = [pl.ds(pl.multiple_of(((cx + 2 * t + n) % NP) * 128, 128), 128) for n in range(2)]
        for head in range(HEADS_HERE):
            here = slice(head * LANES, head * LANES + LANES)
            q = jnp.concatenate([queries[b, here] for b in blocks], axis=0)
            scores = dot_nt(q, keys[:, here])
            top = jnp.max(scores, axis=1, keepdims=True)
            weights = jnp.exp2((scores - top) * (SCALE * LOG2E)).astype(BF)
            got = dot(weights, values[:, here])
            mixed[:, here] = (got / got[:, HD : HD + 1]).astype(BF)
        placed = [dot(mixed[...], p).astype(BF) for p in place]
        for n in range(2):
            e = 2 * t + n
            both = jnp.concatenate([p[n * 128 : n * 128 + 128] for p in placed], axis=0)
            pieces[e * 64 : e * 64 + 64] = dot(gather_slots, both).astype(BF)
            if t < 2:
                continue
            for dy in range(NY):
                y = (sp + dy) % NY
                start(
                    pieces.at[rows16(e * NY + y)], plane_back.at[rows16((e - 4) * NY + sp)],
                    b_send.at[0], b_recv, plane_id((cx + e) % NP, y),
                )

    r, c = iota((256, 256), 0), iota((256, 256), 1)
    turn = onehot(c == (r & 15) * 16 + (r >> 4))

    attend(0)
    attend(1)
    z_back[0:256] = dot(turn, pieces[0:256]).astype(BF)

    def first_z(n, carry):
        i = 15 - n
        start(z_back.at[rows16(i)], back_in.at[rows16(i)], r_send.at[0], rb_recv, z_id((z + NZ - hop(i)) % NZ))
        return carry

    lax.fori_loop(0, 15, first_z, 0)
    back_in[0:16] = z_back[0:16]
    attend(2)
    attend(3)
    waiter(plane_back, 16 * 16, b_send.at[0], b_recv).wait_recv()
    z_back[256:512] = dot(turn, plane_back[...]).astype(BF)

    def second_z(n, carry):
        rows = rows16(31 - n)
        start(z_back.at[rows], final.at[rows], r_send.at[1], r_recv, z_id((z + NZ - hop(15 - n)) % NZ))
        return carry

    lax.fori_loop(0, 15, second_z, 0)
    final[256:272] = z_back[256:272]
    waiter(back_in, 15 * 16, r_send.at[0], rb_recv).wait_recv()
    back_out[...] = dot(turn, back_in[...]).astype(BF)

    def first_plane(k, carry):
        e, y = k // NY, (sp + k % NY) % NY
        to = plane_id((cx + e) % NP, y)
        start(back_out.at[rows16(e * NY + y)], final.at[rows16(e * NY + sp)], b_send.at[1], fb_recv, to)
        return carry

    lax.fori_loop(1, 16, first_plane, 0)
    final[rows16(sp)] = back_out[rows16(sp)]

    f = iota((1, 512), 1)
    e = jnp.where(f < 256, f >> 6, 4 + ((f >> 2) & 3))
    by_y = jnp.where(f < 256, f >> 4, f) & 3
    from_z = (z + hop_of(jnp.where(f < 256, f, f >> 4) & 15)) & (NZ - 1)
    from_owner = (((cx - e) & (NP - 1)) * NZ + from_z).astype(F32)
    mine = jnp.where(owner_cols[:, 0:1] == from_owner, 1.0, 0.0)
    waiter(final, 15 * 16, r_send.at[1], r_recv).wait_recv()
    waiter(final, 15 * 16, b_send.at[1], fb_recv).wait_recv()
    lane = iota((ROWS, PAIR), 1)
    for pair in range(2):
        found = []
        for n in range(2):
            pick = jnp.where(by_y == 2 * pair + n, mine, 0.0).astype(BF)
            got = dot(pick, final[...])
            turned = pltpu.roll(got, PAIR // 2, 1)
            found.append(jnp.where(rank_col == float(n), got, turned))
        back = jnp.where(lane < PAIR // 2, found[0], found[1])
        columns = slice(pair * PAIR, pair * PAIR + PAIR)
        out_ref[:, columns] = (moved[:, columns].astype(F32) + back).astype(BF)

    waiter(outgoing, 7 * 16, n_send.at[0], nz_recv).wait_send()
    waiter(outgoing, 7 * 16, f_send.at[0], fx_recv).wait_send()
    waiter(outgoing, 7 * 16, n_send.at[1], nz_recv).wait_send()
    waiter(outgoing, 8 * 16, f_send.at[1], fx_recv).wait_send()
    waiter(group, 48 * 16, y_send, yx_recv.at[0]).wait_send()
    waiter(pieces, 16 * 16, b_send.at[0], b_recv).wait_send()
    waiter(pieces, 15 * 16, b_send.at[1], b_recv).wait_send()
    waiter(z_back, 15 * 16, r_send.at[0], r_recv).wait_send()
    waiter(z_back, 15 * 16, r_send.at[1], r_recv).wait_send()


def shards(
    patch_qkv, patch_state, window_index, patch_owner, source_request, norm_gain, w_qkv, b_qkv
):
    vmem = pl.BlockSpec(memory_space=pltpu.VMEM)
    hbm = pl.BlockSpec(memory_space=pl.ANY)
    dma = pltpu.SemaphoreType.DMA
    return pl.pallas_call(
        kernel,
        out_shape=jax.ShapeDtypeStruct((ROWS, WIDTH), BF),
        in_specs=[hbm] * 2 + [vmem] * 4 + [hbm, vmem],
        out_specs=vmem,
        scratch_shapes=[
            pltpu.VMEM((3, ROWS, WIDTH), BF),
            pltpu.VMEM((ROWS, WIDTH), BF),
            pltpu.VMEM((1, 3 * PART), F32),
            pltpu.VMEM((ROWS, WIDTH), BF),
            pltpu.VMEM((256, WIDTH), BF),
            pltpu.VMEM((128, WIDTH), BF),
            pltpu.VMEM((128, WIDTH), BF),
            pltpu.VMEM((128, WIDTH), BF),
            pltpu.VMEM((128, WIDTH), BF),
            pltpu.VMEM((1024, WIDTH), BF),
            pltpu.VMEM((3 * PART, WIDTH), BF),
            pltpu.VMEM((1024, LANES), BF),
            pltpu.VMEM((1024, PART), BF),
            pltpu.VMEM((1024, PART), BF),
            pltpu.VMEM((1024, PART), BF),
            pltpu.VMEM((256, PART), BF),
            pltpu.VMEM((512, PAIR), BF),
            pltpu.VMEM((256, PAIR), BF),
            pltpu.VMEM((512, PAIR), BF),
            pltpu.VMEM((256, PAIR), BF),
            pltpu.VMEM((256, PAIR), BF),
            pltpu.VMEM((512, PAIR), BF),
            dma((2,)), dma((12,)), dma((2,)), dma, dma((8,)), dma((2,)), dma, dma((8,)),
            dma, dma((16,)), dma((16,)), dma((16,)),
            dma((2,)), dma, dma, dma((2,)), dma, dma,
        ],
        compiler_params=pltpu.CompilerParams(
            collective_id=0, has_side_effects=True, vmem_limit_bytes=60 * 1024 * 1024
        ),
    )(
        jnp.transpose(patch_qkv, (1, 0, 2)), patch_state, window_index, patch_owner.reshape(1, ROWS), source_request,
        norm_gain, jnp.transpose(w_qkv, (1, 2, 0)), b_qkv,
    )


def solution(mesh):
    in_specs = (
        P(("sec", "sp", "dev"), None, None),
        P(("sec", "sp", "dev"), None),
        P(("sec", "sp", "dev"), None),
        P(("sec", "sp", "dev"), None),
        P(("sec", "dev"), None),
        P(),
        P(None, None, "sp"),
        P(None, "sp"),
    )
    out_specs = P(("sec", "sp", "dev"), None)
    return jax.shard_map(shards, mesh=mesh, in_specs=in_specs, out_specs=out_specs, check_vma=False)
```

```python
import functools

import jax
import jax.numpy as jnp
from jax import lax
from jax.experimental import pallas as pl
from jax.experimental.pallas import tpu as pltpu
from jax.sharding import PartitionSpec as P

HD = 80
NORM_EPS = 1e-06
NZ, NX, NC, NY = 16, 4, 2, 4
NP = NX * NC
ROWS, WIDTH = 128, 1280
LANES = 128
HEADS_HERE = 4
PART = HEADS_HERE * LANES
PAIR = 2 * HEADS_HERE * HD
DEAD = 1024.0
SCALE = HD ** (-0.5)
LOG2E = 1.4426950408889634
MESH = pl.DeviceIdType.MESH
BF, F32, I32 = jnp.bfloat16, jnp.float32, jnp.int32


def hop(i):
    return ((2 * (i % 2) - 1) * ((i + 1) // 2)) % NZ


def hop_of(i):
    return ((2 * (i & 1) - 1) * ((i + 1) >> 1)) & (NZ - 1)


def iota(shape, axis):
    return lax.broadcasted_iota(I32, shape, axis)


def dot(a, b):
    return jnp.dot(a, b, preferred_element_type=F32)


def dot_nt(a, b):
    return lax.dot_general(a, b, (((1,), (1,)), ((), ())), preferred_element_type=F32)


def onehot(mask):
    return jnp.where(mask, 1.0, 0.0).astype(BF)


def rows16(index):
    return pl.ds(pl.multiple_of(index * 16, 16), 16)


def kernel(
    qkv_hbm, state_hbm, order_ref, owner_ref, request_ref, gain_ref, w_hbm, b_ref, out_ref,
    qkv_ref, state_ref, bias_ref,
    moved, outgoing, near_in, near_out, far_in, far_out, group, w_ref, asks, queries, keys, values, mixed,
    pieces, plane_back, z_back, back_in, back_out, final,
    q_sem, w_sem, n_send, nz_recv, nx_recv, f_send, fx_recv, fz_recv, y_send, yl_recv, yr_recv, yx_recv,
    b_send, b_recv, fb_recv, r_send, r_recv, rb_recv,
):
    sec, sp, dev = (lax.axis_index(a) for a in ("sec", "sp", "dev"))
    x, z = dev // NZ, dev % NZ
    cx = sec * NX + x
    right, left = (sp + 1) % NY, (sp + 3) % NY

    load_qkv = pltpu.make_async_copy(qkv_hbm, qkv_ref, q_sem.at[0])
    load_state = pltpu.make_async_copy(state_hbm, state_ref, q_sem.at[1])
    load_w = [
        pltpu.make_async_copy(
            w_hbm.at[part, pl.ds(head * HD, HD)], w_ref.at[pl.ds(part * PART + head * LANES, HD)],
            w_sem.at[part * HEADS_HERE + head],
        )
        for part in range(3)
        for head in range(HEADS_HERE)
    ]
    load_qkv.start()
    load_state.start()
    for load in load_w:
        load.start()

    def plane_id(to_cx, to_y):
        return (to_cx // NX, to_y, (to_cx % NX) * NZ + z)

    def z_id(to_z):
        return (sec, sp, x * NZ + to_z)

    gain = gain_ref[...].reshape(1, WIDTH)
    barrier = pltpu.get_barrier_semaphore()

    def greet_plane(k, carry):
        pl.semaphore_signal(
            barrier, inc=1, device_id=plane_id((cx + k // NY) % NP, (sp + k % NY) % NY), device_id_type=MESH
        )
        return carry

    def greet_z(k, carry):
        pl.semaphore_signal(barrier, inc=1, device_id=z_id((z + k) % NZ), device_id_type=MESH)
        return carry

    lax.fori_loop(1, NP * NY, greet_plane, 0)
    lax.fori_loop(1, NZ, greet_z, 0)

    owner_rows = jnp.broadcast_to(owner_ref[...].astype(F32), (ROWS, ROWS))
    owner_cols = jnp.transpose(owner_rows)
    row_i, col_i = iota((ROWS, ROWS), 0), iota((ROWS, ROWS), 1)
    same = owner_cols == owner_rows
    rank_row = jnp.sum(jnp.where(same & (row_i < col_i), 1.0, 0.0), axis=0, keepdims=True)
    rank_col = jnp.sum(jnp.where(same & (col_i < row_i), 1.0, 0.0), axis=1, keepdims=True)

    order = jnp.broadcast_to(order_ref[...], (ROWS, ROWS))
    in_second = jnp.sum(jnp.where((order == row_i) & (col_i >= 64), 1.0, 0.0), axis=1, keepdims=True)
    second_cols = jnp.broadcast_to(in_second, (ROWS, ROWS))
    same_window = second_cols == jnp.transpose(second_cols)

    def window_half(half, carry):
        base = half * 640
        tiles = [jnp.zeros((ROWS, LANES), F32) for _ in range(5)]
        for head in range(8):
            low, high = head * HD, head * HD + HD
            first, last = low // LANES, (high + LANES - 1) // LANES
            span = (last - first) * LANES
            columns = pl.ds(pl.multiple_of(base + first * LANES, LANES), span)
            lane = iota((ROWS, span), 1) + first * LANES
            mine = (lane >= low) & (lane < high)
            q = qkv_ref[0, :, columns]
            q = jnp.where(mine, q.astype(F32), 0.0).astype(BF)
            scores = dot_nt(q, qkv_ref[1, :, columns])
            scores = jnp.where(same_window, scores * SCALE, -1e30)
            top = jnp.max(scores, axis=1, keepdims=True)
            expo = jnp.exp(scores - top)
            weights = (expo / jnp.sum(expo, axis=1, keepdims=True)).astype(BF)
            got = dot(weights, qkv_ref[2, :, columns])
            got = jnp.where(mine, got, 0.0)
            for t in range(first, last):
                tiles[t] = tiles[t] + got[:, (t - first) * LANES : (t - first + 1) * LANES]
        for t in range(5):
            columns = pl.ds(pl.multiple_of(base + t * LANES, LANES), LANES)
            window_out = tiles[t].astype(BF).astype(F32)
            moved[:, columns] = (state_ref[:, columns].astype(F32) + window_out).astype(BF)
        return carry

    load_qkv.wait()
    load_state.wait()
    lax.fori_loop(0, 2, window_half, 0)

    slot_i = iota((256, ROWS), 0)
    high, low = (slot_i >> 4) & 7, (slot_i >> 1) & 7
    far = slot_i >= 128
    to_z = (z + hop_of(jnp.where(far, 8 + low, high))) & (NZ - 1)
    to_owner = jnp.where(far, high, low) * NZ + to_z
    chosen = (owner_rows[0:1] == to_owner.astype(F32)) & (rank_row == (slot_i & 1).astype(F32))
    picker = onehot(chosen)
    taken = jnp.max(jnp.where(chosen, 1.0, 0.0), axis=1, keepdims=True)
    outgoing[:, 0:LANES] = jnp.where(taken > 0.5, dot(picker, moved[:, 0:LANES]), DEAD).astype(BF)
    outgoing[:, LANES:] = dot(picker, moved[:, LANES:]).astype(BF)

    pl.semaphore_wait(barrier, NP * NY - 1 + NZ - 1)

    def start(src, dst, send_sem, recv_sem, to):
        pltpu.make_async_remote_copy(
            src_ref=src, dst_ref=dst, send_sem=send_sem, recv_sem=recv_sem, device_id=to, device_id_type=MESH
        ).start()

    def waiter(ref, rows, send_sem, recv_sem):
        part = ref.at[pl.ds(0, rows)]
        return pltpu.make_async_remote_copy(
            src_ref=part, dst_ref=part, send_sem=send_sem, recv_sem=recv_sem,
            device_id=(sec, right, dev), device_id_type=MESH,
        )

    def near_z(i, carry):
        rows = rows16(i)
        start(outgoing.at[rows], near_in.at[rows], n_send.at[0], nz_recv, z_id((z + hop(i)) % NZ))
        return carry

    def far_plane(k, carry):
        to = (cx + k) % NP
        start(outgoing.at[rows16(8 + to)], far_in.at[rows16(cx)], f_send.at[0], fx_recv, plane_id(to, sp))
        return carry

    lax.fori_loop(1, 8, near_z, 0)
    lax.fori_loop(1, NP, far_plane, 0)
    far_in[rows16(cx)] = outgoing[rows16(8 + cx)]
    near_in[0:16] = outgoing[0:16]

    r, c = iota((ROWS, ROWS), 0), iota((ROWS, ROWS), 1)
    swap = onehot(c == (r & 7) * 16 + (r >> 4) * 2 + ((r >> 3) & 1))

    waiter(far_in, 7 * 16, f_send.at[0], fx_recv).wait_recv()
    far_out[...] = dot(swap, far_in[...]).astype(BF)

    def far_z(n, carry):
        to = z_id((z + hop(8 + n)) % NZ)
        start(far_out.at[rows16(n)], group.at[rows16(32 + n * NY + sp)], f_send.at[1], fz_recv.at[n], to)
        return carry

    lax.fori_loop(0, 8, far_z, 0)

    waiter(near_in, 7 * 16, n_send.at[0], nz_recv).wait_recv()
    near_out[...] = dot(swap, near_in[...]).astype(BF)

    def near_plane(k, carry):
        to = (cx + k) % NP
        start(near_out.at[rows16(to)], group.at[rows16(cx * NY + sp)], n_send.at[1], nx_recv.at[k], plane_id(to, sp))
        return carry

    lax.fori_loop(1, NP, near_plane, 0)
    group[rows16(cx * NY + sp)] = near_out[rows16(cx)]

    r, c = iota((1024, LANES), 0), iota((1024, LANES), 1)
    high, low = (r >> 6) & 7, r & 7
    source = jnp.where(r < 512, high, low) * NZ + ((z - hop_of(jnp.where(r < 512, low, 8 + high))) & (NZ - 1))
    lane_request = onehot(jnp.broadcast_to(request_ref[...], (LANES, LANES)) == row_i - HD)
    asks[...] = dot_nt(onehot(c == source), lane_request).astype(BF)
    r, c = iota((HEADS_HERE * HD, PART), 0), iota((HEADS_HERE * HD, PART), 1)
    spread = onehot(((c & 127) < HD) & (r == (c >> 7) * HD + (c & 127)))
    for part in range(3):
        bias_ref[:, part * PART : part * PART + PART] = dot(b_ref[part : part + 1], spread)
        for head in range(HEADS_HERE):
            unused = part * PART + head * LANES + HD
            w_ref[unused : unused + LANES - HD] = jnp.zeros((LANES - HD, WIDTH), BF)
    for load in load_w:
        load.wait()

    r, c = iota((256, 256), 0), iota((256, 256), 1)
    by_source = onehot(c == (r & 3) * 64 + ((r >> 2) & 3) * 16 + ((r >> 4) & 1) * 8 + (r >> 5))

    def block(n, y):
        return rows16(((cx + NP - n) % NP if n < 8 else n) * NY + y)

    def send_y(n, from_y, to_y, recv_sem):
        part = group.at[block(n, from_y)]
        start(part, part, y_send, recv_sem, (sec, to_y, dev))

    def wait_one(recv_sem):
        waiter(group, 16, y_send, recv_sem).wait_recv()

    def forward(n):
        if n > 0:
            wait_one(nx_recv.at[n] if n < 8 else fz_recv.at[n - 8])
        send_y(n, sp, right, yl_recv.at[n])
        send_y(n, sp, left, yr_recv.at[n])

    def relay(n):
        if n % 2 == 0:
            wait_one(yl_recv.at[n])
            send_y(n, left, right, yx_recv.at[n])
        else:
            wait_one(yr_recv.at[n])
            send_y(n, right, left, yx_recv.at[n])

    def settle(n):
        wait_one(yr_recv.at[n] if n % 2 == 0 else yl_recv.at[n])
        wait_one(yx_recv.at[n])

    def project(k):
        rows = slice(256 * k, 256 * k + 256)
        raw = group[rows].astype(F32)
        live = raw[:, 0:1] < DEAD / 2
        mean_sq = jnp.mean(raw * raw, axis=1, keepdims=True)
        normed = (raw * lax.rsqrt(mean_sq + NORM_EPS) * gain).astype(BF)
        ask = asks[rows].astype(F32)
        lane = iota((256, LANES), 1)
        shut = jnp.where((lane >= HD) & (lane < HD + 8) & ~((ask > 0.5) & live), -1e30, 0.0)
        ones = jnp.where(lane == HD, 1.0, 0.0)
        for part, extra in enumerate((ask, shut, ones)):
            extra = jnp.concatenate([extra, extra], axis=1)
            for pair in range(2):
                columns = slice(part * PART + pair * 256, part * PART + pair * 256 + 256)
                here = slice(pair * 256, pair * 256 + 256)
                got = (dot_nt(normed, w_ref[columns]) + (bias_ref[:, columns] + extra)).astype(BF)
                if part == 0:
                    if k < 2:
                        for n in range(4):
                            to = (4 * k + n) * 128
                            queries[to : to + 64, here] = got[n * 64 : n * 64 + 64]
                        continue
                    got = dot(by_source, got).astype(BF)
                    for n in range(NP):
                        to = n * 128 + k * 32
                        queries[to : to + 32, here] = got[n * 32 : n * 32 + 32]
                elif part == 1:
                    keys[rows, here] = got
                else:
                    values[rows, here] = got

    for n in range(16):
        forward(n)
        if n >= 2:
            relay(n - 2)
        if n == 14:
            for m in range(8):
                settle(m)
            project(0)
        if n == 15:
            project(1)
    relay(14)
    relay(15)
    for m in range(8, 12):
        settle(m)
    project(2)
    for m in range(12, 16):
        settle(m)
    project(3)

    r, c = iota((PART, PAIR), 0), iota((PART, PAIR), 1)
    spot = (r >> 7) * HD + (r & 127)
    real = (r & 127) < HD
    place = [onehot(real & (c == spot + slot * HEADS_HERE * HD)) for slot in range(2)]
    r, c = iota((64, 256), 0), iota((64, 256), 1)
    slot, y, i = c >> 7, r >> 4, r & 15
    near_row, far_row = y * 16 + slot * 8 + i, 64 + ((i - 8) >> 2) * 32 + slot * 16 + y * 4 + (i & 3)
    gather_slots = onehot((c & 127) == jnp.where(i < 8, near_row, far_row))

    def attend(t):
        blocks = [pl.ds(pl.multiple_of(((cx + 2 * t + n) % NP) * 128, 128), 128) for n in range(2)]
        for head in range(HEADS_HERE):
            here = slice(head * LANES, head * LANES + LANES)
            q = jnp.concatenate([queries[b, here] for b in blocks], axis=0)
            scores = dot_nt(q, keys[:, here])
            top = jnp.max(scores, axis=1, keepdims=True)
            weights = jnp.exp2((scores - top) * (SCALE * LOG2E)).astype(BF)
            got = dot(weights, values[:, here])
            mixed[:, here] = (got / got[:, HD : HD + 1]).astype(BF)
        placed = [dot(mixed[...], p).astype(BF) for p in place]
        for n in range(2):
            e = 2 * t + n
            both = jnp.concatenate([p[n * 128 : n * 128 + 128] for p in placed], axis=0)
            pieces[e * 64 : e * 64 + 64] = dot(gather_slots, both).astype(BF)
            if t < 2:
                continue
            for dy in range(NY):
                y = (sp + dy) % NY
                start(
                    pieces.at[rows16(e * NY + y)], plane_back.at[rows16((e - 4) * NY + sp)],
                    b_send.at[0], b_recv, plane_id((cx + e) % NP, y),
                )

    r, c = iota((256, 256), 0), iota((256, 256), 1)
    turn = onehot(c == (r & 15) * 16 + (r >> 4))

    attend(0)
    attend(1)
    z_back[0:256] = dot(turn, pieces[0:256]).astype(BF)

    def first_z(n, carry):
        i = 15 - n
        start(z_back.at[rows16(i)], back_in.at[rows16(i)], r_send.at[0], rb_recv, z_id((z + NZ - hop(i)) % NZ))
        return carry

    lax.fori_loop(0, 15, first_z, 0)
    back_in[0:16] = z_back[0:16]
    attend(2)
    attend(3)
    waiter(plane_back, 16 * 16, b_send.at[0], b_recv).wait_recv()
    z_back[256:512] = dot(turn, plane_back[...]).astype(BF)

    def second_z(n, carry):
        rows = rows16(31 - n)
        start(z_back.at[rows], final.at[rows], r_send.at[1], r_recv, z_id((z + NZ - hop(15 - n)) % NZ))
        return carry

    lax.fori_loop(0, 15, second_z, 0)
    final[256:272] = z_back[256:272]
    waiter(back_in, 15 * 16, r_send.at[0], rb_recv).wait_recv()
    back_out[...] = dot(turn, back_in[...]).astype(BF)

    def first_plane(k, carry):
        e, y = k // NY, (sp + k % NY) % NY
        to = plane_id((cx + e) % NP, y)
        start(back_out.at[rows16(e * NY + y)], final.at[rows16(e * NY + sp)], b_send.at[1], fb_recv, to)
        return carry

    lax.fori_loop(1, 16, first_plane, 0)
    final[rows16(sp)] = back_out[rows16(sp)]

    f = iota((1, 512), 1)
    e = jnp.where(f < 256, f >> 6, 4 + ((f >> 2) & 3))
    by_y = jnp.where(f < 256, f >> 4, f) & 3
    from_z = (z + hop_of(jnp.where(f < 256, f, f >> 4) & 15)) & (NZ - 1)
    from_owner = (((cx - e) & (NP - 1)) * NZ + from_z).astype(F32)
    mine = jnp.where(owner_cols[:, 0:1] == from_owner, 1.0, 0.0)
    waiter(final, 15 * 16, r_send.at[1], r_recv).wait_recv()
    waiter(final, 15 * 16, b_send.at[1], fb_recv).wait_recv()
    lane = iota((ROWS, PAIR), 1)
    for pair in range(2):
        found = []
        for n in range(2):
            pick = jnp.where(by_y == 2 * pair + n, mine, 0.0).astype(BF)
            got = dot(pick, final[...])
            turned = pltpu.roll(got, PAIR // 2, 1)
            found.append(jnp.where(rank_col == float(n), got, turned))
        back = jnp.where(lane < PAIR // 2, found[0], found[1])
        columns = slice(pair * PAIR, pair * PAIR + PAIR)
        out_ref[:, columns] = (moved[:, columns].astype(F32) + back).astype(BF)

    waiter(outgoing, 7 * 16, n_send.at[0], nz_recv).wait_send()
    waiter(outgoing, 7 * 16, f_send.at[0], fx_recv).wait_send()
    waiter(outgoing, 7 * 16, n_send.at[1], nz_recv).wait_send()
    waiter(outgoing, 8 * 16, f_send.at[1], fx_recv).wait_send()
    waiter(group, 48 * 16, y_send, yx_recv.at[0]).wait_send()
    waiter(pieces, 16 * 16, b_send.at[0], b_recv).wait_send()
    waiter(pieces, 15 * 16, b_send.at[1], b_recv).wait_send()
    waiter(z_back, 15 * 16, r_send.at[0], r_recv).wait_send()
    waiter(z_back, 15 * 16, r_send.at[1], r_recv).wait_send()


def shards(
    patch_qkv, patch_state, window_index, patch_owner, source_request, norm_gain, w_qkv, b_qkv
):
    vmem = pl.BlockSpec(memory_space=pltpu.VMEM)
    hbm = pl.BlockSpec(memory_space=pl.ANY)
    dma = pltpu.SemaphoreType.DMA
    return pl.pallas_call(
        kernel,
        out_shape=jax.ShapeDtypeStruct((ROWS, WIDTH), BF),
        in_specs=[hbm] * 2 + [vmem] * 4 + [hbm, vmem],
        out_specs=vmem,
        scratch_shapes=[
            pltpu.VMEM((3, ROWS, WIDTH), BF),
            pltpu.VMEM((ROWS, WIDTH), BF),
            pltpu.VMEM((1, 3 * PART), F32),
            pltpu.VMEM((ROWS, WIDTH), BF),
            pltpu.VMEM((256, WIDTH), BF),
            pltpu.VMEM((128, WIDTH), BF),
            pltpu.VMEM((128, WIDTH), BF),
            pltpu.VMEM((128, WIDTH), BF),
            pltpu.VMEM((128, WIDTH), BF),
            pltpu.VMEM((1024, WIDTH), BF),
            pltpu.VMEM((3 * PART, WIDTH), BF),
            pltpu.VMEM((1024, LANES), BF),
            pltpu.VMEM((1024, PART), BF),
            pltpu.VMEM((1024, PART), BF),
            pltpu.VMEM((1024, PART), BF),
            pltpu.VMEM((256, PART), BF),
            pltpu.VMEM((512, PAIR), BF),
            pltpu.VMEM((256, PAIR), BF),
            pltpu.VMEM((512, PAIR), BF),
            pltpu.VMEM((256, PAIR), BF),
            pltpu.VMEM((256, PAIR), BF),
            pltpu.VMEM((512, PAIR), BF),
            dma((2,)), dma((12,)), dma((2,)), dma, dma((8,)), dma((2,)), dma, dma((8,)),
            dma, dma((16,)), dma((16,)), dma((16,)),
            dma((2,)), dma, dma, dma((2,)), dma, dma,
        ],
        compiler_params=pltpu.CompilerParams(
            collective_id=0, has_side_effects=True, vmem_limit_bytes=60 * 1024 * 1024
        ),
    )(
        jnp.transpose(patch_qkv, (1, 0, 2)), patch_state, window_index, patch_owner.reshape(1, ROWS), source_request,
        norm_gain, jnp.transpose(w_qkv, (1, 2, 0)), b_qkv,
    )


def solution(mesh):
    in_specs = (
        P(("sec", "sp", "dev"), None, None),
        P(("sec", "sp", "dev"), None),
        P(("sec", "sp", "dev"), None),
        P(("sec", "sp", "dev"), None),
        P(("sec", "dev"), None),
        P(),
        P(None, None, "sp"),
        P(None, "sp"),
    )
    out_specs = P(("sec", "sp", "dev"), None)
    return jax.shard_map(shards, mesh=mesh, in_specs=in_specs, out_specs=out_specs, check_vma=False)
```
